32 devices in a mesh: row: 8 (over y, x, core), col: 4 (over z).
Axes of the slice: x: 2, y: 2, z: 4, core: 2. Of those that a mesh axis runs over, the one named last changes fastest.
Arguments:
- amplitudes: float32 [65536, 256], P(None, ('row', 'col')), may hold values from -6 to 6
- integrals: float32 [5632, 65536], P('row', 'col'), may hold values from -0.0234375 to 0.0234375
Outputs:
- ladder: float32 [5632, 256], P('row', 'col')
The draws below stay inside these ranges and needn't reach their ends.
All inputs are finite; a program needn't handle non-finite values.
Results may differ from the reference program's by a relative error of at most 0.00007.
Values sent between devices are 32-bit elements; how exact they have to be, the bound alone decides.
No kernel may reach another device: no remote copies, remote signals or barrier semaphores. Data moves between devices by JAX's collectives and lax.ppermute only.
A program may use at most 128 MiB of HBM per device.

```python
import jax
import jax.numpy as jnp
from jax import lax

IJ = 256
CD = 65536
AB = 5632


def with_spikes(values, stream_key, source, target, blocks, factor):
    def block_of(position):
        return (jnp.arange(values.shape[position]) // (values.shape[position] // blocks)).reshape((-1,) + (1,) * (values.ndim - 1 - position))

    one_side = jax.random.permutation(stream_key, blocks)[block_of(target)]
    far = (block_of(target) + blocks // 2) % blocks
    return jnp.where((block_of(source) == one_side) | (block_of(source) == far), factor * values, values)


def block_levels(rng, dims, cuts, smallest, largest):
    factor_of = 1.0
    for axis_at, parts in cuts:
        heights = jax.random.uniform(jax.random.fold_in(jax.random.fold_in(rng, 6), axis_at), (parts,), jnp.float32, smallest / len(cuts), largest / len(cuts))
        factor_of = factor_of * jnp.repeat(jnp.exp(heights), dims[axis_at] // parts).reshape((-1,) + (1,) * (len(dims) - 1 - axis_at))
    return factor_of


def gaussian(rng, extent, deviation, reach, cuts=(), dtype=jnp.bfloat16):
    result = deviation * jax.random.normal(rng, extent, jnp.float32)
    if cuts:
        result = result * block_levels(rng, extent, cuts, -0.22, 0.18)
    return jnp.clip(result, -reach, reach).astype(dtype)


def gaussian_with(rng, dims, spread, reach, split, heavy, held_as=jnp.bfloat16):
    entries = spread * jax.random.normal(rng, dims, jnp.float32)
    if split:
        entries = entries * block_levels(rng, dims, split, -0.22, 0.18)
    return jnp.clip(with_spikes(entries, jax.random.fold_in(rng, 3), *heavy), -reach, reach).astype(held_as)


def setup_inputs(seed: int = 0) -> dict:
    keys = jax.random.split(jax.random.key(seed), 3)
    amplitudes = gaussian_with(keys[0], (CD, IJ), 1.0, 6.0, ((1, 32),), (0, 1, 32, 2.75), jnp.float32)
    integrals = gaussian(keys[1], (AB, CD), CD ** -0.5, 0.0234375, ((0, 8), (1, 4)), jnp.float32)
    return {"amplitudes": amplitudes, "integrals": integrals}


def reference(amplitudes, integrals):
    contracted = jnp.dot(integrals, amplitudes, preferred_element_type=jnp.float32, precision=lax.Precision.HIGHEST)
    return 0.5 * contracted
```

```python
import functools

import jax
import jax.numpy as jnp
from jax import lax
from jax.experimental import pallas as pl
from jax.experimental.pallas import tpu as pltpu
from jax.sharding import PartitionSpec as P

F32, BF16 = jnp.float32, jnp.bfloat16
NT = (((1,), (1,)), ((), ()))
SUB, LANE = 8, 128

PARTS = (3, 3, 2)
TILE, LIMIT = 2048, 28
COST = 3


def split(x):
    hi = x.astype(BF16)
    return hi, (x - hi.astype(F32)).astype(BF16)


def product(v, t):
    dot = lambda a, b: lax.dot_general(a, b, NT, preferred_element_type=F32)
    vh, vl = split(v)
    th, tl = split(t)
    return dot(vh, th) + (dot(vh, tl) + dot(vl, th))


def kernel(where, v_ref, *refs, groups, cols, lanes, acc, last):
    step = pl.program_id(0)
    if last:
        out_ref, tau, total = refs[-3:]
    else:
        out_ref, tau = refs[-2:]
        total = out_ref
    chip, core, col = where[0], where[1], where[2]
    for g, distances in enumerate(groups):
        for other in range(2):
            ref = refs[2 * g + other]
            its = core if other == 0 else 1 - core
            one, two = its + 1, 2 - its
            for m, source in enumerate((chip, chip ^ one, chip ^ two, chip ^ 3)):
                for k, d in enumerate(distances):
                    at = ((source * 2 + its) * cols + (col ^ d)) * lanes
                    tau[pl.ds(pl.multiple_of(at, lanes), lanes), :] = ref[pl.ds((m * len(distances) + k) * lanes, lanes), :]
    new = product(v_ref[...], tau[...])

    @pl.when(step == 0)
    def _():
        total[...] = new + refs[2 * len(groups)][...] if acc else new

    @pl.when(step > 0)
    def _():
        total[...] += new

    if last:

        @pl.when(step == pl.num_programs(0) - 1)
        def _():
            rows = total.shape[0]
            out_ref[:, :rows] = total[...].T
            if rows < out_ref.shape[1]:
                out_ref[:, rows:] = jnp.zeros((out_ref.shape[0], out_ref.shape[1] - rows), F32)


def multiply(where, v, quads, groups, acc, at, width, tile, cols, lanes, last):
    rows, ij = v.shape[0], 8 * lanes * cols
    whole = pl.BlockSpec((rows, ij), lambda i, w: (0, 0))
    specs, operands = [pl.BlockSpec((rows, tile), lambda i, w: (0, i + at // tile))], [v]
    for own, theirs, begin in quads:
        for a in (own, theirs):
            specs.append(pl.BlockSpec((a.shape[0], tile), lambda i, w, b=begin: (0, i + (at - b) // tile)))
            operands.append(a)
    if acc is not None:
        specs.append(whole)
        operands.append(acc)
    scratch = [pltpu.VMEM((ij, tile), F32)]
    if last:
        shape = (ij, pl.cdiv(rows, LANE) * LANE)
        spec = pl.BlockSpec(shape, lambda i, w: (0, 0))
        scratch.append(pltpu.VMEM((rows, ij), F32))
    else:
        shape, spec = (rows, ij), whole
    return pl.pallas_call(
        functools.partial(kernel, groups=groups, cols=cols, lanes=lanes, acc=acc is not None, last=last),
        grid_spec=pltpu.PrefetchScalarGridSpec(
            num_scalar_prefetch=1, grid=(width // tile,), in_specs=specs, out_specs=spec, scratch_shapes=scratch
        ),
        out_shape=jax.ShapeDtypeStruct(shape, F32),
        input_output_aliases={len(operands): 0} if acc is not None and not last else {},
        cost_estimate=pl.CostEstimate(
            flops=COST * 6 * rows * ij * width, bytes_accessed=COST * 4 * (rows + ij) * width, transcendentals=0
        ),
        compiler_params=pltpu.CompilerParams(vmem_limit_bytes=LIMIT << 20),
    )(where, *operands)


def xor(n, bits):
    return [(i, i ^ bits) for i in range(n)]


def pipelined(amplitudes, integrals):
    tau = amplitudes.T
    lanes, (height, block) = tau.shape[0], integrals.shape
    row, col = lax.axis_index("row"), lax.axis_index("col")
    rows, cols = lax.axis_size("row"), lax.axis_size("col")
    where = jnp.stack([row // 2, row % 2, col]).astype(jnp.int32)
    near = [(i, i ^ (2 if i % 2 == 0 else 4)) for i in range(rows)]
    far = [(i, i ^ (4 if i % 2 == 0 else 2)) for i in range(rows)]
    parts = [p * block // 8 for p in PARTS]
    begins = [sum(parts[:i]) for i in range(len(parts))]
    seen = []
    piece, first, both, quad, theirs, gone = {}, {}, {}, {}, {}, {}
    acc = None

    def send(x, axis, pairs):
        return lax.ppermute(lax.optimization_barrier((x, *seen))[0], axis, pairs)

    def cut(d, begin, width):
        return lax.dynamic_slice(tau, (0, (col ^ d) * block + begin), (lanes, width))

    def along(u):
        if u == 1:
            gone[u] = [send(cut(1, 0, block), "col", xor(cols, 1))]
        else:
            gone[u] = [send(cut(d, begins[u - 2], parts[u - 2]), "col", xor(cols, d)) for d in range(2, cols)]
        piece[u] = jnp.concatenate(gone[u], 0)

    def to_near(u):
        first[u] = send(piece[u], "row", near)

    def to_far(u):
        pair = jnp.concatenate([piece[u], first[u]], 0)
        both[u] = send(pair, "row", far)
        quad[u] = jnp.concatenate([pair, both[u]], 0)

    def swap(u):
        theirs[u] = send(quad[u], "row", xor(rows, 1))

    def multiply_part(u):
        nonlocal acc
        quads = [(quad[0], theirs[0], 0), (quad[1], theirs[1], 0), (quad[u], theirs[u], begins[u - 2])]
        groups = ((0,), (1,), tuple(range(2, cols)))
        last = u == len(parts) + 1
        acc = multiply(where, integrals, quads, groups, acc, begins[u - 2], parts[u - 2], TILE, cols, lanes, last)
        seen.append(acc)

    piece[0] = cut(0, 0, block)
    to_near(0)
    along(1)
    seen.append(first[0])
    to_far(0)
    along(2)
    seen.extend(gone[1])
    to_near(1)
    seen.append(both[0])
    swap(0)
    seen.append(first[1])
    to_far(1)
    seen.extend(gone[2])
    to_near(2)
    along(3)
    seen.append(both[1])
    swap(1)
    seen.append(first[2])
    to_far(2)
    seen.append(theirs[0])
    seen.append(theirs[1])
    seen.extend(gone[3])
    to_near(3)
    along(4)
    seen.append(both[2])
    swap(2)
    seen.append(first[3])
    to_far(3)
    seen.append(theirs[2])
    seen.extend(gone[4])
    to_near(4)
    seen.append(both[3])
    swap(3)
    seen.append(first[4])
    to_far(4)
    multiply_part(2)
    seen.append(theirs[3])
    seen.append(both[4])
    swap(4)
    multiply_part(3)
    seen.append(theirs[4])
    multiply_part(4)
    share = acc.shape[0] // cols
    mine = lambda c: lax.dynamic_slice(acc, (c * share, 0), (share, acc.shape[1]))
    got = [send(mine(col ^ d), "col", xor(cols, d)) for d in range(1, cols)]
    out = mine(col)
    for g in got:
        out = out + g
    return (0.5 * out[:, :height]).T


def plain(amplitudes, integrals):
    panel = lax.all_to_all(amplitudes, "col", split_axis=0, concat_axis=1, tiled=True)
    panel = lax.all_gather(panel, "row", axis=1, tiled=True)
    partial = jnp.dot(integrals, panel, preferred_element_type=F32, precision=lax.Precision.HIGH)
    return 0.5 * lax.psum_scatter(partial, "col", scatter_dimension=1, tiled=True)


def solution(mesh):
    rows, cols = mesh.shape["row"], mesh.shape["col"]

    def per_device(amplitudes, integrals):
        lanes, block = amplitudes.shape[1], integrals.shape[1]
        fits = rows == 8 and cols == 4 and lanes % SUB == 0 and block % (TILE * 8) == 0 and lanes * rows * cols % LANE == 0
        return (pipelined if fits else plain)(amplitudes, integrals)

    return jax.shard_map(
        per_device,
        mesh=mesh,
        in_specs=(P(None, ("row", "col")), P("row", "col")),
        out_specs=P("row", "col"),
        check_vma=False,
    )
```

```python
import functools

import jax
import jax.numpy as jnp
from jax import lax
from jax.experimental import pallas as pl
from jax.experimental.pallas import tpu as pltpu
from jax.sharding import PartitionSpec as P

F32, BF16 = jnp.float32, jnp.bfloat16
NT = (((1,), (1,)), ((), ()))
SUB, LANE, MXU = 8, 128, 256

PARTS = (3, 3, 2)
TILE, LIMIT = 2048, 28
COST = 3


def split(x):
    hi = x.astype(BF16)
    return hi, (x - hi.astype(F32)).astype(BF16)


def product(v, t):
    dot = lambda a, b: lax.dot_general(a, b, NT, preferred_element_type=F32)
    vh, vl = split(v)
    th, tl = split(t)
    n = t.shape[0]
    if 2 * n <= MXU:
        wide = dot(vh, jnp.concatenate([th, tl], 0))
        return wide[:, :n] + (wide[:, n:] + dot(vl, th))
    return dot(vh, th) + (dot(vh, tl) + dot(vl, th))


def kernel(where, v_ref, *refs, groups, lanes, acc, last):
    step = pl.program_id(0)
    if last:
        out_ref, tau, total = refs[-3:]
    else:
        out_ref, tau = refs[-2:]
        total = out_ref
    chip, core = where[0], where[1]
    for g, (half, begin, planes) in enumerate(groups):
        for other in range(2):
            its = core if other == 0 else 1 - core
            one, two = its + 1, 2 - its
            for m, source in enumerate((chip, chip ^ one, chip ^ two, chip ^ 3)):
                at = half * 16 * lanes + ((source * 2 + its) * 2 + begin) * lanes
                size = planes * lanes
                ref = refs[4 * g + 2 * other + m // 2]
                tau[pl.ds(pl.multiple_of(at, lanes), size), :] = ref[pl.ds(m % 2 * size, size), :]
    new = product(v_ref[...], tau[...])

    @pl.when(step == 0)
    def _():
        total[...] = new + refs[4 * len(groups)][...] if acc else new

    @pl.when(step > 0)
    def _():
        total[...] += new

    if last:

        @pl.when(step == pl.num_programs(0) - 1)
        def _():
            rows = total.shape[0]
            out_ref[:, :rows] = total[...].T
            if rows < out_ref.shape[1]:
                out_ref[:, rows:] = jnp.zeros((out_ref.shape[0], out_ref.shape[1] - rows), F32)


def multiply(where, v, quads, acc, at, width, tile, lanes, last):
    rows = v.shape[0]
    groups = tuple(q[0] for q in quads)
    ij = len({g[0] for g in groups}) * 16 * lanes
    lowest = min(g[0] for g in groups)
    groups = tuple((half - lowest, begin, planes) for half, begin, planes in groups)
    specs, operands = [pl.BlockSpec((rows, tile), lambda i, w: (0, i + at // tile))], [v]
    for _, pieces, begin in quads:
        for a in pieces:
            specs.append(pl.BlockSpec((a.shape[0], tile), lambda i, w, b=begin: (0, i + (at - b) // tile)))
            operands.append(a)
    if acc is not None:
        specs.append(pl.BlockSpec((rows, ij), lambda i, w: (0, acc[1])))
        operands.append(acc[0])
    scratch = [pltpu.VMEM((ij, tile), F32)]
    if last:
        shape = (ij, pl.cdiv(rows, LANE) * LANE)
        spec = pl.BlockSpec(shape, lambda i, w: (0, 0))
        scratch.append(pltpu.VMEM((rows, ij), F32))
    else:
        shape, spec = (rows, ij), pl.BlockSpec((rows, ij), lambda i, w: (0, 0))
    return pl.pallas_call(
        functools.partial(kernel, groups=groups, lanes=lanes, acc=acc is not None, last=last),
        grid_spec=pltpu.PrefetchScalarGridSpec(
            num_scalar_prefetch=1, grid=(width // tile,), in_specs=specs, out_specs=spec, scratch_shapes=scratch
        ),
        out_shape=jax.ShapeDtypeStruct(shape, F32),
        cost_estimate=pl.CostEstimate(
            flops=COST * 6 * rows * ij * width, bytes_accessed=COST * 4 * (rows + ij) * width, transcendentals=0
        ),
        compiler_params=pltpu.CompilerParams(vmem_limit_bytes=LIMIT << 20),
    )(where, *operands)


def xor(n, bits):
    return [(i, i ^ bits) for i in range(n)]


def pipelined(amplitudes, integrals):
    tau = amplitudes.T
    lanes, (height, block) = tau.shape[0], integrals.shape
    row, col = lax.axis_index("row"), lax.axis_index("col")
    rows, cols = lax.axis_size("row"), lax.axis_size("col")
    where = jnp.stack([row // 2, row % 2]).astype(jnp.int32)
    near = [(i, i ^ (2 if i % 2 == 0 else 4)) for i in range(rows)]
    far = [(i, i ^ (4 if i % 2 == 0 else 2)) for i in range(rows)]
    parts = [p * block // 8 for p in PARTS]
    begins = [sum(parts[:i]) for i in range(len(parts) + 1)]
    seen = []
    piece, first, pair, both, their_pair, their_both, gone = {}, {}, {}, {}, {}, {}, {}
    totals, sums = [None, None], [None, None]

    def send(x, axis, pairs):
        return lax.ppermute(lax.optimization_barrier((x, *seen))[0], axis, pairs)

    def cut(d, begin, width):
        return lax.dynamic_slice(tau, (0, (col ^ d) * block + begin), (lanes, width))

    def along(u):
        if u == 1:
            gone[u] = [send(cut(1, 0, block), "col", xor(cols, 1))]
        else:
            gone[u] = [send(cut(d, begins[u - 2], parts[u - 2]), "col", xor(cols, d)) for d in range(2, cols)]
        piece[u] = jnp.concatenate(gone[u], 0)

    def to_near(u):
        first[u] = send(piece[u], "row", near)
        pair[u] = jnp.concatenate([piece[u], first[u]], 0)

    def to_far(u):
        both[u] = send(pair[u], "row", far)

    def swap_pair(u):
        their_pair[u] = send(pair[u], "row", xor(rows, 1))

    def swap_both(u):
        their_both[u] = send(both[u], "row", xor(rows, 1))

    def have(u):
        return pair[u], both[u], their_pair[u], their_both[u]

    def times(halves, begin, width):
        quads = []
        if 0 in halves:
            quads += [((0, u, 1), have(u), 0) for u in (0, 1)]
        if 1 in halves:
            u = begins.index(begin) + 2
            quads.append(((1, 0, 2), have(u), begin))
        last = begin + width == block
        acc = multiply(where, integrals, quads, totals[halves[0]], begin, width, TILE, lanes, last)
        for place, half in enumerate(halves):
            totals[half] = (acc, place)
        seen.append(acc)

    def add_up(half):
        acc, place = totals[half]
        share = 4 * lanes
        mine = lambda c: lax.dynamic_slice(acc, ((place * cols + c) * share, 0), (share, acc.shape[1]))
        sums[half] = [mine(col)] + [send(mine(col ^ d), "col", xor(cols, d)) for d in range(1, cols)]

    piece[0] = cut(0, 0, block)
    to_near(0)
    along(1)
    seen.append(first[0])
    to_far(0)
    swap_pair(0)
    along(2)
    seen.extend(gone[1])
    to_near(1)
    seen.append(both[0])
    swap_both(0)
    seen.append(first[1])
    to_far(1)
    swap_pair(1)
    seen.extend(gone[2])
    to_near(2)
    along(3)
    seen.append(both[1])
    swap_both(1)
    seen.append(first[2])
    to_far(2)
    swap_pair(2)
    seen.append(their_pair[0])
    seen.append(their_both[0])
    seen.append(their_pair[1])
    seen.append(their_both[1])
    seen.extend(gone[3])
    to_near(3)
    along(4)
    seen.append(both[2])
    swap_both(2)
    seen.append(first[3])
    to_far(3)
    swap_pair(3)
    seen.append(their_pair[2])
    seen.append(their_both[2])
    seen.extend(gone[4])
    to_near(4)
    times((0, 1), begins[0], parts[0])
    seen.append(first[4])
    to_far(4)
    swap_pair(4)
    seen.append(both[3])
    swap_both(3)
    seen.append(their_pair[3])
    seen.append(their_both[3])
    times((0, 1), begins[1], parts[1])
    seen.append(both[4])
    swap_both(4)
    seen.append(their_pair[4])
    seen.append(their_both[4])
    times((0,), begins[2], parts[2])
    add_up(0)
    times((1,), begins[2], parts[2])
    add_up(1)
    planes = [[] for _ in range(cols)]
    for half in range(2):
        for s in range(cols):
            x = sums[half][s].reshape(2, 2, lanes, -1)
            for k in range(2):
                planes[s ^ (2 * half + k)].append(x[:, k])
    out = [0.5 * functools.reduce(jnp.add, p) for p in planes]
    low, high = (col & 1) == 1, (col & 2) == 2
    out = [jnp.where(low, out[d ^ 1], out[d]) for d in range(cols)]
    out = [jnp.where(high, out[d ^ 2], out[d]) for d in range(cols)]
    return jnp.stack(out, 1).reshape(2 * cols * lanes, -1)[:, :height].T


def plain(amplitudes, integrals):
    panel = lax.all_to_all(amplitudes, "col", split_axis=0, concat_axis=1, tiled=True)
    panel = lax.all_gather(panel, "row", axis=1, tiled=True)
    partial = jnp.dot(integrals, panel, preferred_element_type=F32, precision=lax.Precision.HIGH)
    return 0.5 * lax.psum_scatter(partial, "col", scatter_dimension=1, tiled=True)


def solution(mesh):
    rows, cols = mesh.shape["row"], mesh.shape["col"]

    def per_device(amplitudes, integrals):
        lanes, block = amplitudes.shape[1], integrals.shape[1]
        fits = rows == 8 and cols == 4 and lanes % SUB == 0 and block % (TILE * 8) == 0 and lanes * rows * cols % LANE == 0
        return (pipelined if fits else plain)(amplitudes, integrals)

    return jax.shard_map(
        per_device,
        mesh=mesh,
        in_specs=(P(None, ("row", "col")), P("row", "col")),
        out_specs=P("row", "col"),
        check_vma=False,
    )
```

```python
import functools

import jax
import jax.numpy as jnp
from jax import lax
from jax.experimental import pallas as pl
from jax.experimental.pallas import tpu as pltpu
from jax.sharding import PartitionSpec as P

F32, BF16 = jnp.float32, jnp.bfloat16
NT = (((1,), (1,)), ((), ()))
SUB, LANE, MXU = 8, 128, 256

PARTS = (3, 3, 2)
TILE, LIMIT = 2048, 22
COST = 3


def split(x):
    hi = x.astype(BF16)
    return hi, (x - hi.astype(F32)).astype(BF16)


def product(v, t):
    dot = lambda a, b: lax.dot_general(a, b, NT, preferred_element_type=F32)
    vh, vl = split(v)
    th, tl = split(t)
    n = t.shape[0]
    if 2 * n <= MXU:
        wide = dot(vh, jnp.concatenate([th, tl], 0))
        return wide[:, :n] + (wide[:, n:] + dot(vl, th))
    return dot(vh, th) + (dot(vh, tl) + dot(vl, th))


def kernel(where, v_ref, *refs, groups, lanes, acc, last, tile, skips, held):
    step = pl.program_id(0)
    if last:
        out_ref, tau, total = refs[-3:]
    else:
        out_ref, tau = refs[-2:]
        total = out_ref
    chip, core = where[0], where[1]
    for g, (half, begin, planes) in enumerate(groups):
        for other in range(2):
            its = core if other == 0 else 1 - core
            one, two = its + 1, 2 - its
            for m, source in enumerate((chip, chip ^ one, chip ^ two, chip ^ 3)):
                at = half * 16 * lanes + ((source * 2 + its) * 2 + begin) * lanes
                size = planes * lanes
                ref = refs[4 * g + 2 * other + m // 2]
                here = pl.ds(pl.multiple_of(skips[g] + step * tile, tile), tile)
                tau[pl.ds(pl.multiple_of(at, lanes), size), :] = ref[pl.ds(m % 2 * size, size), here]
    v = v_ref[:, pl.ds(pl.multiple_of(step * tile, tile), tile)] if held else v_ref[...]
    new = product(v, tau[...])

    @pl.when(step == 0)
    def _():
        total[...] = new + refs[4 * len(groups)][...] if acc else new

    @pl.when(step > 0)
    def _():
        total[...] += new

    if last:

        @pl.when(step == pl.num_programs(0) - 1)
        def _():
            rows = total.shape[0]
            out_ref[:, :rows] = total[...].T
            if rows < out_ref.shape[1]:
                out_ref[:, rows:] = jnp.zeros((out_ref.shape[0], out_ref.shape[1] - rows), F32)


def multiply(where, v, quads, acc, at, width, tile, lanes, last, held):
    rows = v.shape[0]
    groups = tuple(q[0] for q in quads)
    ij = len({g[0] for g in groups}) * 16 * lanes
    lowest = min(g[0] for g in groups)
    groups = tuple((half - lowest, begin, planes) for half, begin, planes in groups)
    if held:
        specs, operands = [pl.BlockSpec(memory_space=pltpu.VMEM)], [v]
    else:
        specs, operands = [pl.BlockSpec((rows, tile), lambda i, w: (0, i + at // tile))], [v]
    for _, pieces, _ in quads:
        for a in pieces:
            specs.append(pl.BlockSpec(memory_space=pltpu.VMEM))
            operands.append(pltpu.with_memory_space_constraint(a, pltpu.VMEM))
    if acc is not None:
        specs.append(pl.BlockSpec((rows, ij), lambda i, w: (0, acc[1])))
        operands.append(acc[0])
    skips = tuple(at - begin for _, _, begin in quads)
    scratch = [pltpu.VMEM((ij, tile), F32)]
    if last:
        shape = (ij, pl.cdiv(rows, LANE) * LANE)
        spec = pl.BlockSpec(shape, lambda i, w: (0, 0))
        scratch.append(pltpu.VMEM((rows, ij), F32))
    else:
        shape, spec = (rows, ij), pl.BlockSpec((rows, ij), lambda i, w: (0, 0))
    return pl.pallas_call(
        functools.partial(kernel, groups=groups, lanes=lanes, acc=acc is not None, last=last, tile=tile, skips=skips, held=held),
        grid_spec=pltpu.PrefetchScalarGridSpec(
            num_scalar_prefetch=1, grid=(width // tile,), in_specs=specs, out_specs=spec, scratch_shapes=scratch
        ),
        out_shape=jax.ShapeDtypeStruct(shape, F32),
        cost_estimate=pl.CostEstimate(
            flops=COST * 6 * rows * ij * width, bytes_accessed=COST * 4 * (rows + ij) * width, transcendentals=0
        ),
        compiler_params=pltpu.CompilerParams(vmem_limit_bytes=LIMIT << 20),
    )(where, *operands)


def xor(n, bits):
    return [(i, i ^ bits) for i in range(n)]


def pipelined(amplitudes, integrals):
    tau = amplitudes.T
    lanes, (height, block) = tau.shape[0], integrals.shape
    row, col = lax.axis_index("row"), lax.axis_index("col")
    rows, cols = lax.axis_size("row"), lax.axis_size("col")
    where = jnp.stack([row // 2, row % 2]).astype(jnp.int32)
    near = [(i, i ^ (2 if i % 2 == 0 else 4)) for i in range(rows)]
    far = [(i, i ^ (4 if i % 2 == 0 else 2)) for i in range(rows)]
    parts = [p * block // 8 for p in PARTS]
    begins = [sum(parts[:i]) for i in range(len(parts) + 1)]
    seen = []
    piece, first, pair, both, their_pair, their_both, gone = {}, {}, {}, {}, {}, {}, {}
    held = {}
    totals, sums = [None, None], [None, None]

    def send(x, axis, pairs):
        return lax.ppermute(lax.optimization_barrier((x, *seen))[0], axis, pairs)

    def cut(d, begin, width):
        return lax.dynamic_slice(tau, (0, (col ^ d) * block + begin), (lanes, width))

    def along(u):
        if u == 1:
            gone[u] = [send(cut(1, 0, block), "col", xor(cols, 1))]
        else:
            gone[u] = [send(cut(d, begins[u - 2], parts[u - 2]), "col", xor(cols, d)) for d in range(2, cols)]
        piece[u] = jnp.concatenate(gone[u], 0)

    def to_near(u):
        first[u] = send(piece[u], "row", near)
        pair[u] = jnp.concatenate([piece[u], first[u]], 0)

    def to_far(u):
        both[u] = send(pair[u], "row", far)

    def swap_pair(u):
        their_pair[u] = send(pair[u], "row", xor(rows, 1))

    def swap_both(u):
        their_both[u] = send(both[u], "row", xor(rows, 1))

    def have(u):
        return pair[u], both[u], their_pair[u], their_both[u]

    def hold(u):
        begin = begins[u - 2]
        v = lax.optimization_barrier((integrals, *seen))[0]
        v = lax.slice(v, (0, begin), (height, begin + parts[u - 2]))
        held[begin] = pltpu.with_memory_space_constraint(v, pltpu.VMEM)
        seen.append(held[begin])

    def times(halves, begin, width):
        quads = []
        if 0 in halves:
            quads += [((0, u, 1), have(u), 0) for u in (0, 1)]
        if 1 in halves:
            u = begins.index(begin) + 2
            quads.append(((1, 0, 2), have(u), begin))
        last = begin + width == block
        v = held.get(begin)
        acc = multiply(
            where, integrals if v is None else v, quads, totals[halves[0]], begin, width, TILE, lanes, last, v is not None
        )
        for place, half in enumerate(halves):
            totals[half] = (acc, place)
        seen.append(acc)

    def add_up(half):
        acc, place = totals[half]
        share = 4 * lanes
        mine = lambda c: lax.dynamic_slice(acc, ((place * cols + c) * share, 0), (share, acc.shape[1]))
        sums[half] = [mine(col)] + [send(mine(col ^ d), "col", xor(cols, d)) for d in range(1, cols)]

    piece[0] = cut(0, 0, block)
    to_near(0)
    along(1)
    seen.append(first[0])
    to_far(0)
    swap_pair(0)
    along(2)
    seen.extend(gone[1])
    to_near(1)
    hold(4)
    seen.append(both[0])
    swap_both(0)
    seen.append(first[1])
    to_far(1)
    swap_pair(1)
    seen.extend(gone[2])
    to_near(2)
    seen.append(their_pair[1])
    along(3)
    seen.append(both[1])
    swap_both(1)
    seen.append(first[2])
    to_far(2)
    swap_pair(2)
    seen.append(their_pair[0])
    seen.append(their_both[0])
    seen.append(their_pair[1])
    seen.append(their_both[1])
    seen.extend(gone[3])
    to_near(3)
    along(4)
    seen.append(both[2])
    swap_both(2)
    seen.append(first[3])
    to_far(3)
    swap_pair(3)
    seen.append(their_pair[2])
    seen.append(their_both[2])
    seen.extend(gone[4])
    to_near(4)
    times((0, 1), begins[0], parts[0])
    seen.append(first[4])
    to_far(4)
    swap_pair(4)
    seen.append(both[3])
    swap_both(3)
    seen.append(their_pair[3])
    seen.append(their_both[3])
    times((0, 1), begins[1], parts[1])
    seen.append(both[4])
    swap_both(4)
    seen.append(their_pair[4])
    seen.append(their_both[4])
    times((0,), begins[2], parts[2])
    add_up(0)
    times((1,), begins[2], parts[2])
    add_up(1)
    planes = [[] for _ in range(cols)]
    for half in range(2):
        for s in range(cols):
            x = sums[half][s].reshape(2, 2, lanes, -1)
            for k in range(2):
                planes[s ^ (2 * half + k)].append(x[:, k])
    out = [0.5 * functools.reduce(jnp.add, p) for p in planes]
    low, high = (col & 1) == 1, (col & 2) == 2
    out = [jnp.where(low, out[d ^ 1], out[d]) for d in range(cols)]
    out = [jnp.where(high, out[d ^ 2], out[d]) for d in range(cols)]
    return jnp.stack(out, 1).reshape(2 * cols * lanes, -1)[:, :height].T


def plain(amplitudes, integrals):
    panel = lax.all_to_all(amplitudes, "col", split_axis=0, concat_axis=1, tiled=True)
    panel = lax.all_gather(panel, "row", axis=1, tiled=True)
    partial = jnp.dot(integrals, panel, preferred_element_type=F32, precision=lax.Precision.HIGH)
    return 0.5 * lax.psum_scatter(partial, "col", scatter_dimension=1, tiled=True)


def solution(mesh):
    rows, cols = mesh.shape["row"], mesh.shape["col"]

    def per_device(amplitudes, integrals):
        lanes, block = amplitudes.shape[1], integrals.shape[1]
        fits = rows == 8 and cols == 4 and lanes % SUB == 0 and block % (TILE * 8) == 0 and lanes * rows * cols % LANE == 0
        return (pipelined if fits else plain)(amplitudes, integrals)

    return jax.shard_map(
        per_device,
        mesh=mesh,
        in_specs=(P(None, ("row", "col")), P("row", "col")),
        out_specs=P("row", "col"),
        check_vma=False,
    )
```

```python
import functools

import jax
import jax.numpy as jnp
from jax import lax
from jax.experimental import pallas as pl
from jax.experimental.pallas import tpu as pltpu
from jax.sharding import PartitionSpec as P

F32, BF16 = jnp.float32, jnp.bfloat16
NT = (((1,), (1,)), ((), ()))
SUB, LANE, MXU = 8, 128, 256

PARTS = (3, 3, 2)
TILE, STEP, LIMIT = 2048, 2048, 22
COST = 3


def split(x):
    hi = x.astype(BF16)
    return hi, (x - hi.astype(F32)).astype(BF16)


def product(v, t):
    dot = lambda a, b: lax.dot_general(a, b, NT, preferred_element_type=F32)
    vh, vl = split(v)
    th, tl = split(t)
    n = t.shape[0]
    if 2 * n <= MXU:
        wide = dot(vh, jnp.concatenate([th, tl], 0))
        return wide[:, :n] + (wide[:, n:] + dot(vl, th))
    return dot(vh, th) + (dot(vh, tl) + dot(vl, th))


def kernel(where, v_ref, *refs, groups, lanes, acc, last, tile, skips, held):
    step = pl.program_id(0)
    if last:
        out_ref, tau, total = refs[-3:]
    else:
        out_ref, tau = refs[-2:]
        total = out_ref
    chip, core = where[0], where[1]
    for g, (half, begin, planes) in enumerate(groups):
        for other in range(2):
            its = core if other == 0 else 1 - core
            one, two = its + 1, 2 - its
            for m, source in enumerate((chip, chip ^ one, chip ^ two, chip ^ 3)):
                at = half * 16 * lanes + ((source * 2 + its) * 2 + begin) * lanes
                size = planes * lanes
                ref = refs[4 * g + 2 * other + m // 2]
                here = pl.ds(pl.multiple_of(skips[g] + step * tile, tile), tile)
                tau[pl.ds(pl.multiple_of(at, lanes), size), :] = ref[pl.ds(m % 2 * size, size), here]
    v = v_ref[:, pl.ds(pl.multiple_of(step * tile, tile), tile)] if held else v_ref[...]
    new = product(v, tau[...])

    @pl.when(step == 0)
    def _():
        total[...] = new + refs[4 * len(groups)][...] if acc else new

    @pl.when(step > 0)
    def _():
        total[...] += new

    if last:

        @pl.when(step == pl.num_programs(0) - 1)
        def _():
            rows = total.shape[0]
            out_ref[:, :rows] = total[...].T
            if rows < out_ref.shape[1]:
                out_ref[:, rows:] = jnp.zeros((out_ref.shape[0], out_ref.shape[1] - rows), F32)


def multiply(where, v, quads, acc, at, width, tile, lanes, last, held):
    rows = v.shape[0]
    groups = tuple(q[0] for q in quads)
    ij = len({g[0] for g in groups}) * 16 * lanes
    lowest = min(g[0] for g in groups)
    groups = tuple((half - lowest, begin, planes) for half, begin, planes in groups)
    if held:
        specs, operands = [pl.BlockSpec(memory_space=pltpu.VMEM)], [v]
    else:
        specs, operands = [pl.BlockSpec((rows, tile), lambda i, w: (0, i + at // tile))], [v]
    for _, pieces, _ in quads:
        for a in pieces:
            specs.append(pl.BlockSpec(memory_space=pltpu.VMEM))
            operands.append(pltpu.with_memory_space_constraint(a, pltpu.VMEM))
    if acc is not None:
        specs.append(pl.BlockSpec((rows, ij), lambda i, w: (0, acc[1])))
        operands.append(acc[0])
    skips = tuple(at - begin for _, _, begin in quads)
    scratch = [pltpu.VMEM((ij, tile), F32)]
    if last:
        shape = (ij, pl.cdiv(rows, LANE) * LANE)
        spec = pl.BlockSpec(shape, lambda i, w: (0, 0))
        scratch.append(pltpu.VMEM((rows, ij), F32))
    else:
        shape, spec = (rows, ij), pl.BlockSpec((rows, ij), lambda i, w: (0, 0))
    return pl.pallas_call(
        functools.partial(kernel, groups=groups, lanes=lanes, acc=acc is not None, last=last, tile=tile, skips=skips, held=held),
        grid_spec=pltpu.PrefetchScalarGridSpec(
            num_scalar_prefetch=1, grid=(width // tile,), in_specs=specs, out_specs=spec, scratch_shapes=scratch
        ),
        out_shape=jax.ShapeDtypeStruct(shape, F32),
        cost_estimate=pl.CostEstimate(
            flops=COST * 6 * rows * ij * width, bytes_accessed=COST * 4 * (rows + ij) * width, transcendentals=0
        ),
        compiler_params=pltpu.CompilerParams(vmem_limit_bytes=LIMIT << 20),
    )(where, *operands)


def xor(n, bits):
    return [(i, i ^ bits) for i in range(n)]


def pipelined(amplitudes, integrals):
    tau = amplitudes.T
    lanes, (height, block) = tau.shape[0], integrals.shape
    row, col = lax.axis_index("row"), lax.axis_index("col")
    rows, cols = lax.axis_size("row"), lax.axis_size("col")
    where = jnp.stack([row // 2, row % 2]).astype(jnp.int32)
    near = [(i, i ^ (2 if i % 2 == 0 else 4)) for i in range(rows)]
    far = [(i, i ^ (4 if i % 2 == 0 else 2)) for i in range(rows)]
    parts = [p * block // 8 for p in PARTS]
    begins = [sum(parts[:i]) for i in range(len(parts) + 1)]
    seen = []
    piece, first, pair, both, their_pair, their_both, gone = {}, {}, {}, {}, {}, {}, {}
    held = {}
    totals, sums = [None, None], [None, None]

    def send(x, axis, pairs):
        return lax.ppermute(lax.optimization_barrier((x, *seen))[0], axis, pairs)

    def cut(d, begin, width):
        return lax.dynamic_slice(tau, (0, (col ^ d) * block + begin), (lanes, width))

    def along(u):
        if u == 1:
            gone[u] = [send(cut(1, 0, block), "col", xor(cols, 1))]
        else:
            gone[u] = [send(cut(d, begins[u - 2], parts[u - 2]), "col", xor(cols, d)) for d in range(2, cols)]
        piece[u] = jnp.concatenate(gone[u], 0)

    def to_near(u):
        first[u] = send(piece[u], "row", near)
        pair[u] = jnp.concatenate([piece[u], first[u]], 0)

    def to_far(u):
        both[u] = send(pair[u], "row", far)

    def swap_pair(u):
        their_pair[u] = send(pair[u], "row", xor(rows, 1))

    def swap_both(u):
        their_both[u] = send(both[u], "row", xor(rows, 1))

    def have(u):
        return pair[u], both[u], their_pair[u], their_both[u]

    def hold(u):
        begin = begins[u - 2]
        v = lax.optimization_barrier((integrals, *seen))[0]
        v = lax.slice(v, (0, begin), (height, begin + parts[u - 2]))
        held[begin] = pltpu.with_memory_space_constraint(v, pltpu.VMEM)
        seen.append(held[begin])

    def times(halves, begin, width):
        quads = []
        if 0 in halves:
            quads += [((0, u, 1), have(u), 0) for u in (0, 1)]
        if 1 in halves:
            u = begins.index(begin) + 2
            quads.append(((1, 0, 2), have(u), begin))
        last = begin + width == block
        v = held.get(begin)
        acc = multiply(
            where, integrals if v is None else v, quads, totals[halves[0]], begin, width, STEP if v is None else TILE, lanes, last, v is not None
        )
        for place, half in enumerate(halves):
            totals[half] = (acc, place)
        seen.append(acc)

    def add_up(half):
        acc, place = totals[half]
        share = 4 * lanes
        mine = lambda c: lax.dynamic_slice(acc, ((place * cols + c) * share, 0), (share, acc.shape[1]))
        sums[half] = [mine(col)] + [send(mine(col ^ d), "col", xor(cols, d)) for d in range(1, cols)]

    piece[0] = cut(0, 0, block)
    tau = lax.optimization_barrier((tau, piece[0]))[0]
    to_near(0)
    along(1)
    seen.append(first[0])
    to_far(0)
    swap_pair(0)
    along(2)
    seen.extend(gone[1])
    to_near(1)
    hold(4)
    seen.append(both[0])
    swap_both(0)
    seen.append(first[1])
    to_far(1)
    swap_pair(1)
    seen.extend(gone[2])
    to_near(2)
    seen.append(their_pair[1])
    along(3)
    seen.append(both[1])
    swap_both(1)
    seen.append(first[2])
    to_far(2)
    swap_pair(2)
    seen.append(their_pair[0])
    seen.append(their_both[0])
    seen.append(their_pair[1])
    seen.append(their_both[1])
    seen.extend(gone[3])
    to_near(3)
    along(4)
    seen.append(both[2])
    swap_both(2)
    seen.append(first[3])
    to_far(3)
    swap_pair(3)
    seen.append(their_pair[2])
    seen.append(their_both[2])
    seen.extend(gone[4])
    to_near(4)
    times((0, 1), begins[0], parts[0])
    seen.append(first[4])
    to_far(4)
    swap_pair(4)
    seen.append(both[3])
    swap_both(3)
    seen.append(their_pair[3])
    seen.append(their_both[3])
    times((0, 1), begins[1], parts[1])
    seen.append(both[4])
    swap_both(4)
    seen.append(their_pair[4])
    seen.append(their_both[4])
    times((0,), begins[2], parts[2])
    add_up(0)
    times((1,), begins[2], parts[2])
    add_up(1)
    planes = [[] for _ in range(cols)]
    for half in range(2):
        for s in range(cols):
            x = sums[half][s].reshape(2, 2, lanes, -1)
            for k in range(2):
                planes[s ^ (2 * half + k)].append(x[:, k])
    out = [0.5 * functools.reduce(jnp.add, p) for p in planes]
    low, high = (col & 1) == 1, (col & 2) == 2
    out = [jnp.where(low, out[d ^ 1], out[d]) for d in range(cols)]
    out = [jnp.where(high, out[d ^ 2], out[d]) for d in range(cols)]
    return jnp.stack(out, 1).reshape(2 * cols * lanes, -1)[:, :height].T


def plain(amplitudes, integrals):
    panel = lax.all_to_all(amplitudes, "col", split_axis=0, concat_axis=1, tiled=True)
    panel = lax.all_gather(panel, "row", axis=1, tiled=True)
    partial = jnp.dot(integrals, panel, preferred_element_type=F32, precision=lax.Precision.HIGH)
    return 0.5 * lax.psum_scatter(partial, "col", scatter_dimension=1, tiled=True)


def solution(mesh):
    rows, cols = mesh.shape["row"], mesh.shape["col"]

    def per_device(amplitudes, integrals):
        lanes, block = amplitudes.shape[1], integrals.shape[1]
        fits = rows == 8 and cols == 4 and lanes % SUB == 0 and block % (TILE * 8) == 0 and lanes * rows * cols % LANE == 0
        return (pipelined if fits else plain)(amplitudes, integrals)

    return jax.shard_map(
        per_device,
        mesh=mesh,
        in_specs=(P(None, ("row", "col")), P("row", "col")),
        out_specs=P("row", "col"),
        check_vma=False,
    )
```
